32 devices in a mesh: stretch: 8 (over z, y), section: 4 (over x, core).
Axes of the slice: x: 2, y: 2, z: 4, core: 2. Of those that a mesh axis runs over, the one named last changes fastest.
Arguments:
- hidden: bfloat16 [4, 4096, 4096], P('section', 'stretch'), may hold values from -64 to 64
- norm_gain: float32 [4, 4096], P('section'), may hold values from 0.5 to 1.5
- queries: bfloat16 [4, 4096, 2048], P('section', 'stretch'), may hold values from -110 to 110
- cache: bfloat16 [4, 128, 32, 4096], P('section', 'stretch'), may hold values from -35 to 35
- nbr_shard: int32 [64, 2], P('stretch'), may hold values from 0 to 7, as said below
- nbr_slot: int32 [64, 2], P('stretch'), may hold values from 0 to 15
- grad_heads: bfloat16 [4, 4096, 2048], P('section', 'stretch'), may hold values from -24 to 24
- grad_out: bfloat16 [4, 4096, 4096], P('section', 'stretch'), may hold values from -3 to 3
- query_weight: bfloat16 [4, 4096, 2048], P('section', 'stretch'), may hold values from -0.09375 to 0.09375
Outputs:
- section_grads: bfloat16 [4, 4096, 4096], P('section', 'stretch')
The draws below stay inside these ranges and needn't reach their ends.
Inputs may be any that keep to these rules, and one draw needn't show every extreme that they name: `nbr_shard`: the 2 shards of a stretch differ. In the 8 stretches of one device (aligned blocks of rows) no shard is named more than 2 times; one shard is named exactly 2 times in every such block.
All inputs are finite; a program needn't handle non-finite values.
Results may differ from the reference program's by a relative error of at most 0.0067.
Values may be sent and summed in bfloat16 or wider, within the bound.
A program may use at most 192 MiB of HBM per device.

```python
import math
import jax
import jax.numpy as jnp
from jax import lax

D = 4096
HEADS = 16
HEAD_DIM = 128
STRETCH = 64
NBRS = 2
NBR_LEN = 32
CH_DEV = 8
DB_DEV = 16
QW = 2048
SHARDS = 8
CAP = 2
LAYERS = 4
STRETCHES = 64
TOKENS = 4096
DB_ROWS = 128


def draw_hidden(key, part):
    row_key, col_key, noise_key = jax.random.split(key, 3)
    row_scale = jnp.exp(jax.random.uniform(row_key, (LAYERS, TOKENS, 1), minval=math.log(0.3), maxval=math.log(3.0)))
    col_scale = jnp.exp(jax.random.uniform(col_key, (1, 1, D), minval=math.log(0.3), maxval=math.log(3.0)))
    base_noise = jax.random.normal(noise_key, (LAYERS, TOKENS, D))
    return (base_noise * row_scale * col_scale).astype(jnp.bfloat16)


def draw_queries(key, part):
    base_noise = jax.random.normal(key, (LAYERS, TOKENS, QW))
    return base_noise.astype(jnp.bfloat16)


def draw_cache(key, part):
    noise_key = jax.random.fold_in(key, 0)
    base_noise = jax.random.normal(noise_key, (LAYERS, DB_ROWS, NBR_LEN, 2 * QW))
    return base_noise.astype(jnp.bfloat16)


def draw_nbr_shard(key, part):
    hot_shard = jax.random.randint(jax.random.fold_in(key, 11), (), 0, SHARDS)
    request_count = NBRS * CH_DEV

    def one_block(block_key):
        perm_key, roll_key = jax.random.split(block_key)
        shuffled = jax.random.permutation(perm_key, SHARDS - 1).astype(jnp.int32)
        others = shuffled + (shuffled >= hot_shard).astype(jnp.int32)
        seq_pos = jnp.arange(request_count)
        group_idx = jnp.minimum(jnp.maximum(seq_pos - CAP, 0) // CAP, SHARDS - 2)
        owners = jnp.where(seq_pos < CAP, hot_shard, others[group_idx])
        offset = jax.random.randint(roll_key, (), 0, request_count)
        owners = jnp.roll(owners, offset)
        return owners.reshape(NBRS, CH_DEV).T
    block_keys = jax.random.split(jax.random.fold_in(key, 12), STRETCHES // CH_DEV)
    return jax.vmap(one_block)(block_keys).reshape(STRETCHES, NBRS).astype(jnp.int32)


def place_ends(values, key, smallest, largest):
    longest = values.shape.index(max(values.shape))
    spots = []
    for shift in (0, 1):
        where = [jax.random.randint(jax.random.fold_in(key, axis), (), 0, length) for axis, length in enumerate(values.shape)]
        where[longest] = (where[longest] + shift) % values.shape[longest]
        spots.append(tuple(where))
    return values.at[spots[0]].set(smallest).at[spots[1]].set(largest)


def shard_levels(own_key, shape, pieces, smallest, largest):
    loudness, own = 1.0, jax.random.fold_in(own_key, 6)
    for dim, shards_of in pieces:
        draws = jnp.exp(jax.random.uniform(jax.random.fold_in(own, dim), (shards_of,), jnp.float32, smallest / len(pieces), largest / len(pieces)))
        loudness = loudness * jnp.repeat(draws, shape[dim] // shards_of).reshape([-1 if axis == dim else 1 for axis in range(len(shape))])
    return loudness


def scatter_about(own_key, shape, scale, reach, pieces=(), kind=jnp.bfloat16):
    level = shard_levels(own_key, shape, pieces, -0.22, 0.18) if pieces else 1.0
    array = jax.random.normal(own_key, shape, jnp.float32) * scale * level
    return jnp.minimum(jnp.maximum(array, -reach), reach).astype(kind)


def setup_inputs(seed: int = 0) -> dict:
    key_list = jax.random.split(jax.random.key(seed), 10)
    hidden = draw_hidden(jax.random.fold_in(key_list[9], 71), 0)
    norm_gain = jnp.clip(0.5 + 1.0 * jax.random.uniform(key_list[1], (LAYERS, D), jnp.float32) ** shard_levels(key_list[1], (LAYERS, D), ((0, 4),), -0.2, 0.2), 0.5, 1.5)
    queries = draw_queries(jax.random.fold_in(key_list[9], 71), 0)
    cache = draw_cache(jax.random.fold_in(key_list[9], 71), 0)
    nbr_shard = draw_nbr_shard(jax.random.fold_in(key_list[9], 71), 0)
    nbr_slot = place_ends(jax.random.randint(key_list[5], (STRETCHES, NBRS), 0, DB_DEV), jax.random.fold_in(key_list[5], 1), 0, DB_DEV - 1).astype(jnp.int32)
    grad_heads = scatter_about(key_list[6], (LAYERS, TOKENS, QW), 4.0, 24.0, ((0, 4), (1, 8)))
    grad_out = scatter_about(key_list[7], (LAYERS, TOKENS, D), 0.5, 3.0, ((0, 4), (1, 8)))
    query_weight = scatter_about(key_list[8], (LAYERS, D, QW), D ** -0.5, 0.09375, ((0, 4), (1, 8)))
    return {"hidden": hidden, "norm_gain": norm_gain, "queries": queries, "cache": cache, "nbr_shard": nbr_shard, "nbr_slot": nbr_slot, "grad_heads": grad_heads, "grad_out": grad_out, "query_weight": query_weight}


norm_eps = 1e-05

def layer_grad(hidden, gain, queries, cache, rows, head_grads, out_grad, weight):
    factor = HEAD_DIM ** (-0.5)
    fetched = cache[rows].reshape(STRETCHES, NBRS * NBR_LEN, 2 * QW)
    key_heads = fetched[:, :, :QW].reshape(STRETCHES, NBRS * NBR_LEN, HEADS, HEAD_DIM).astype(jnp.float32)
    value_heads = fetched[:, :, QW:].reshape(STRETCHES, NBRS * NBR_LEN, HEADS, HEAD_DIM).astype(jnp.float32)
    query_heads = queries.reshape(STRETCHES, STRETCH, HEADS, HEAD_DIM).astype(jnp.float32)
    grad_split = head_grads.reshape(STRETCHES, STRETCH, HEADS, HEAD_DIM).astype(jnp.float32)
    scores = jnp.einsum('cqhd,ckhd->chqk', query_heads, key_heads) * factor
    row_max = lax.optimization_barrier(jnp.max(scores, axis=-1, keepdims=True))
    exp_scores = jnp.exp(scores - row_max)
    attn_probs = exp_scores / lax.optimization_barrier(jnp.sum(exp_scores, axis=-1, keepdims=True))
    dprob = jnp.einsum('cqhd,ckhd->chqk', grad_split, value_heads)
    row_inner = lax.optimization_barrier(jnp.sum(attn_probs * dprob, axis=-1, keepdims=True))
    dscore = (factor * attn_probs * (dprob - row_inner)).astype(jnp.bfloat16)
    query_grad = jnp.einsum('chqk,ckhd->cqhd', dscore.astype(jnp.float32), key_heads)
    query_grad = query_grad.astype(jnp.bfloat16).reshape(TOKENS, QW)
    norm_grad = jnp.dot(query_grad, weight.T, preferred_element_type=jnp.float32)
    values_in = hidden.astype(jnp.float32)
    inv_rms = lax.rsqrt(lax.optimization_barrier(jnp.mean(values_in * values_in, axis=-1, keepdims=True)) + norm_eps)
    normed = values_in * inv_rms
    scaled_grad = norm_grad * gain[None, :]
    mean_term = lax.optimization_barrier(jnp.mean(scaled_grad * normed, axis=-1, keepdims=True))
    return out_grad.astype(jnp.float32) + inv_rms * (scaled_grad - normed * mean_term)

def reference(hidden, norm_gain, queries, cache, nbr_shard, nbr_slot, grad_heads, grad_out, query_weight):
    rows = (nbr_shard * DB_DEV + nbr_slot).astype(jnp.int32)
    results = []
    for layer in range(LAYERS):
        results.append(layer_grad(hidden[layer], norm_gain[layer], queries[layer], cache[layer], rows, grad_heads[layer], grad_out[layer], query_weight[layer]))
    stacked = jnp.stack(results, axis=0)
    return jnp.roll(stacked, -1, axis=0).astype(jnp.bfloat16)
```

```python
import functools

import jax
import jax.numpy as jnp
from jax import lax
from jax.experimental import pallas as pl
from jax.experimental.pallas import tpu as pltpu
from jax.sharding import PartitionSpec as P

HEAD_DIM = 128
STRETCH = 64
MESH = pl.DeviceIdType.MESH
NT = (((1,), (1,)), ((), ()))
NN = (((1,), (0,)), ((), ()))

norm_eps = 1e-05


def slot_ranks(owners):
    count = owners.shape[0]
    positions = jnp.arange(count)
    same_owner = owners[:, None] == owners[None, :]
    earlier = positions[:, None] > positions[None, :]
    return jnp.sum((same_owner & earlier).astype(jnp.int32), axis=1)


def request_table(owners, slot_rank, slot_ids, shards, capacity):
    matched = (owners[:, None, None] == jnp.arange(shards)[None, :, None]) & (
        slot_rank[:, None, None] == jnp.arange(capacity)[None, None, :]
    )
    return jnp.sum(jnp.where(matched, slot_ids[:, None, None], 0), axis=0)


def kernel(
    shards, sections, capacity, parts,
    wanted, place, gain, hidden, queries, cache, grads, grad_out, weight,
    out,
    req, req_s, cache_v, picked, fetched, q_v, gh_v, wbuf, qg, stage, g_in, hid_in, gout_in,
    load_sem, req_send, req_recv, kv_send, kv_recv, w_send, w_recv, qg_send, qg_recv,
    g_send, g_recv, x_send, x_recv, out_sem,
):
    me = lax.axis_index("stretch")
    sec = lax.axis_index("section")
    before = lax.rem(sec + sections - 1, sections)
    after = lax.rem(sec + 1, sections)
    side = lax.rem(me, 2)
    spot = me // 2
    partner = me + 1 - 2 * side
    line = shards // 2
    tokens, qwidth = queries.shape
    width = hidden.shape[1]
    heads = qwidth // HEAD_DIM
    stretches = tokens // STRETCH
    span = cache.shape[1]
    piece = weight.shape[0] // parts

    def remote(src, dst, ssem, rsem, stretch, section):
        return pltpu.make_async_remote_copy(
            src_ref=src, dst_ref=dst, send_sem=ssem, recv_sem=rsem,
            device_id=(stretch, section), device_id_type=MESH,
        )

    cache_load = pltpu.make_async_copy(cache, cache_v, load_sem.at[0])
    q_load = pltpu.make_async_copy(queries, q_v, load_sem.at[1])
    gh_load = pltpu.make_async_copy(grads, gh_v, load_sem.at[2])
    cache_load.start()

    barrier = pltpu.get_barrier_semaphore()

    @pl.loop(1, shards)
    def _(off):
        pl.semaphore_signal(
            barrier, inc=1, device_id=(lax.rem(me + off, shards), sec), device_id_type=MESH
        )

    for section in (before, after):
        for stretch in (me, partner):
            pl.semaphore_signal(barrier, inc=1, device_id=(stretch, section), device_id_type=MESH)
    pl.semaphore_wait(barrier, shards + 3)

    def req_copy(to, slot):
        return remote(wanted.at[to], req.at[slot], req_send.at[to], req_recv.at[slot], to, sec)

    @pl.loop(1, shards)
    def _(off):
        req_copy(lax.rem(me + off, shards), me).start()

    q_load.start()
    gh_load.start()
    own_loads = [
        pltpu.make_async_copy(
            weight.at[pl.ds(c * piece, piece)], wbuf.at[spot * parts + c], load_sem.at[4 + c]
        )
        for c in range(parts)
    ]
    for load in own_loads:
        load.start()
    req[me] = wanted[me]
    cache_load.wait()

    @pl.loop(1, shards)
    def _(off):
        req_copy(lax.rem(me + off, shards), lax.rem(me + off, shards)).wait_recv()

    req_load = pltpu.make_async_copy(req, req_s, load_sem.at[3])
    req_load.start()
    req_load.wait()

    def kv_copy(to, slot):
        return remote(
            picked.at[pl.ds(to * capacity, capacity)],
            fetched.at[pl.ds(slot * capacity, capacity)],
            kv_send.at[to], kv_recv.at[slot], to, sec,
        )

    @pl.loop(1, shards)
    def _(off):
        to = lax.rem(me + off, shards)
        for k in range(capacity):
            picked[to * capacity + k] = cache_v[req_s[to, 0, k]]
        kv_copy(to, me).start()

    for k in range(capacity):
        fetched[me * capacity + k] = cache_v[req_s[me, 0, k]]

    def w_copy(way, block, c):
        unit = block * parts + c
        return remote(
            wbuf.at[unit], wbuf.at[unit], w_send.at[way, unit], w_recv.at[unit],
            me + (2 if way else -2), sec,
        )

    for c in range(parts):
        own_loads[c].wait()

        @pl.when(spot < line - 1)
        def _():
            w_copy(1, spot, c).start()

        @pl.when(spot > 0)
        def _():
            w_copy(0, spot, c).start()

    hid_copy = remote(hidden, hid_in, x_send.at[0], x_recv.at[0], me, before)
    gout_copy = remote(grad_out, gout_in, x_send.at[1], x_recv.at[1], me, before)
    hid_copy.start()
    gout_copy.start()

    def take(dist, c):
        @pl.when(spot - dist >= 0)
        def _():
            w_copy(1, spot - dist, c).wait_recv()

            @pl.when(spot < line - 1)
            def _():
                w_copy(1, spot - dist, c).start()

        @pl.when(spot + dist < line)
        def _():
            w_copy(0, spot + dist, c).wait_recv()

            @pl.when(spot > 0)
            def _():
                w_copy(0, spot + dist, c).start()

    for c in range(parts):
        if line > 2:
            take(1, c)

    @pl.loop(1, shards)
    def _(off):
        source = lax.rem(me + off, shards)
        kv_copy(source, source).wait_recv()

    q_load.wait()
    gh_load.wait()
    factor = HEAD_DIM ** (-0.5)

    def qg_copy(c):
        rows = pl.ds(c * STRETCH, STRETCH)
        return remote(
            qg.at[0, rows], qg.at[1, rows], qg_send.at[c], qg_recv.at[c], partner, sec
        )

    @pl.loop(0, stretches)
    def _(c):
        rows = pl.ds(pl.multiple_of(c * STRETCH, STRETCH), STRETCH)
        first, second = place[c, 0], place[c, 1]
        for h in range(heads):
            cols = slice(h * HEAD_DIM, (h + 1) * HEAD_DIM)
            vcols = slice(qwidth + h * HEAD_DIM, qwidth + (h + 1) * HEAD_DIM)
            keys = jnp.concatenate([fetched[first, :, cols], fetched[second, :, cols]], axis=0)
            values = jnp.concatenate([fetched[first, :, vcols], fetched[second, :, vcols]], axis=0)
            scores = lax.dot_general(
                q_v[rows, cols], keys, NT, preferred_element_type=jnp.float32
            ) * factor
            dprob = lax.dot_general(
                gh_v[rows, cols], values, NT, preferred_element_type=jnp.float32
            )
            exps = jnp.exp(scores - jnp.max(scores, axis=-1, keepdims=True))
            probs = exps / jnp.sum(exps, axis=-1, keepdims=True)
            inner = jnp.sum(probs * dprob, axis=-1, keepdims=True)
            dscore = (factor * probs * (dprob - inner)).astype(jnp.bfloat16)
            qg[0, rows, cols] = lax.dot_general(
                dscore, keys, NN, preferred_element_type=jnp.float32
            ).astype(jnp.bfloat16)
        qg_copy(c).start()

    @pl.loop(0, stretches)
    def _(c):
        qg_copy(c).wait_recv()

    def g_copy(which, block, c):
        unit = (block * 2 + side) * parts + c
        return remote(
            stage.at[which, block * parts + c], g_in.at[unit],
            g_send.at[which, block * parts + c], g_recv.at[unit],
            partner if which else me, before,
        )

    def work(block, c):
        unit = block * parts + c
        scale = gain[(block * 2 + side) * parts + c]
        for which in (1, 0):
            product = lax.dot_general(
                qg[which], wbuf[unit], NT, preferred_element_type=jnp.float32
            )
            stage[which, unit] = (product * scale).astype(jnp.bfloat16)
            g_copy(which, block, c).start()

    @pl.loop(0, parts)
    def _(c):
        work(spot, c)

    @pl.loop(1, line)
    def _(dist):
        @pl.when(dist + 1 < line - 1)
        def _():
            for c in range(parts):
                take(dist + 1, c)

        @pl.loop(0, parts)
        def _(c):
            @pl.when(dist == line - 1)
            def _():
                take(dist, c)

            @pl.loop(0, 2)
            def _(way):
                block = spot + dist * (2 * way - 1)

                @pl.when((block >= 0) & (block < line))
                def _():
                    work(block, c)

    hid_copy.wait_recv()
    gout_copy.wait_recv()
    units = shards * parts

    @pl.loop(0, units)
    def _(unit):
        remote(
            stage.at[0, 0], g_in.at[unit], g_send.at[0, 0], g_recv.at[unit], me, before
        ).wait_recv()

    tile = 32
    tiles = tokens // tile

    def out_copy(i):
        rows = pl.ds(i * tile, tile)
        return pltpu.make_async_copy(gout_in.at[rows], out.at[rows], out_sem.at[i])

    @pl.loop(0, tiles)
    def _(i):
        rows = pl.ds(pl.multiple_of(i * tile, tile), tile)
        squares = jnp.zeros((tile, piece), jnp.float32)
        inners = jnp.zeros((tile, piece), jnp.float32)
        for unit in range(units):
            x = hid_in[rows, unit * piece:(unit + 1) * piece].astype(jnp.float32)
            g = g_in[unit, rows, :].astype(jnp.float32)
            squares += x * x
            inners += g * x
        inv = lax.rsqrt(jnp.sum(squares, axis=-1, keepdims=True) / width + norm_eps)
        mean = jnp.sum(inners, axis=-1, keepdims=True) * inv / width
        slope = inv * inv * mean
        for unit in range(units):
            cols = slice(unit * piece, (unit + 1) * piece)
            x = hid_in[rows, cols].astype(jnp.float32)
            g = g_in[unit, rows, :].astype(jnp.float32)
            total = gout_in[rows, cols].astype(jnp.float32) + (inv * g - slope * x)
            gout_in[rows, cols] = total.astype(jnp.bfloat16)
        out_copy(i).start()

    @pl.loop(1, shards)
    def _(off):
        to = lax.rem(me + off, shards)
        req_copy(to, me).wait_send()
        kv_copy(to, me).wait_send()

    hid_copy.wait_send()
    gout_copy.wait_send()

    @pl.loop(0, stretches)
    def _(c):
        qg_copy(c).wait_send()

    @pl.loop(0, line)
    def _(block):
        for c in range(parts):
            g_copy(0, block, c).wait_send()
            g_copy(1, block, c).wait_send()

            @pl.when((block <= spot) & (spot < line - 1))
            def _():
                w_copy(1, block, c).wait_send()

            @pl.when((block >= spot) & (spot > 0))
            def _():
                w_copy(0, block, c).wait_send()

    @pl.loop(0, tiles)
    def _(i):
        out_copy(i).wait()


def local(
    sections, hidden, norm_gain, queries, cache, nbr_shard, nbr_slot, grad_heads, grad_out,
    query_weight,
):
    shards = lax.axis_size("stretch")
    _, tokens, qwidth = queries.shape
    width = hidden.shape[2]
    stretches, neighbours = nbr_shard.shape
    capacity = (neighbours * stretches + shards - 1) // shards
    _, slots, span, _ = cache.shape
    owners = nbr_shard.reshape(-1)
    slot_rank = slot_ranks(owners)
    wanted = request_table(owners, slot_rank, nbr_slot.reshape(-1), shards, capacity)
    wanted = jnp.pad(wanted[:, None, :], ((0, 0), (0, 7), (0, 128 - capacity)))
    place = (owners * capacity + slot_rank).reshape(stretches, neighbours)
    rows = query_weight.shape[1]
    parts = 2 if rows % 512 == 0 else 1
    piece = rows // parts
    line = shards // 2
    units = shards * parts
    bf16 = jnp.bfloat16
    dma = pltpu.SemaphoreType.DMA
    vmem = pl.BlockSpec(memory_space=pltpu.VMEM)
    hbm = pl.BlockSpec(memory_space=pl.ANY)
    out = pl.pallas_call(
        functools.partial(kernel, shards, sections, capacity, parts),
        out_shape=jax.ShapeDtypeStruct((tokens, width), bf16),
        in_specs=[vmem, pl.BlockSpec(memory_space=pltpu.SMEM), vmem] + [hbm] * 6,
        out_specs=hbm,
        scratch_shapes=[
            pltpu.VMEM((shards, 8, 128), jnp.int32),
            pltpu.SMEM((shards, 8, 128), jnp.int32),
            pltpu.VMEM((slots, span, 2 * qwidth), bf16),
            pltpu.VMEM((shards * capacity, span, 2 * qwidth), bf16),
            pltpu.VMEM((shards * capacity, span, 2 * qwidth), bf16),
            pltpu.VMEM((tokens, qwidth), bf16),
            pltpu.VMEM((tokens, qwidth), bf16),
            pltpu.VMEM((line * parts, piece, qwidth), bf16),
            pltpu.VMEM((2, tokens, qwidth), bf16),
            pltpu.VMEM((2, line * parts, tokens, piece), bf16),
            pltpu.VMEM((units, tokens, piece), bf16),
            pltpu.VMEM((tokens, width), bf16),
            pltpu.VMEM((tokens, width), bf16),
            dma((4 + parts,)),
            dma((shards,)),
            dma((shards,)),
            dma((shards,)),
            dma((shards,)),
            dma((2, line * parts)),
            dma((line * parts,)),
            dma((stretches,)),
            dma((stretches,)),
            dma((2, line * parts)),
            dma((units,)),
            dma((2,)),
            dma((2,)),
            dma((tokens // 32,)),
        ],
        compiler_params=pltpu.CompilerParams(
            collective_id=0, has_side_effects=True, vmem_limit_bytes=60 * 1024 * 1024
        ),
        cost_estimate=pl.CostEstimate(
            flops=2 * tokens * qwidth * width, bytes_accessed=24 << 20, transcendentals=0
        ),
    )(
        wanted, place, norm_gain[0].reshape(units, 1, piece), hidden[0], queries[0], cache[0],
        grad_heads[0], grad_out[0], query_weight[0],
    )
    return out[None]


def solution(mesh):
    in_specs = (
        P("section", "stretch", None),
        P("section", None),
        P("section", "stretch", None),
        P("section", "stretch", None, None),
        P("stretch", None),
        P("stretch", None),
        P("section", "stretch", None),
        P("section", "stretch", None),
        P("section", "stretch", None),
    )
    return jax.shard_map(
        functools.partial(local, mesh.shape["section"]), mesh=mesh, in_specs=in_specs,
        out_specs=P("section", "stretch", None), check_vma=False,
    )
```

```python
import functools

import jax
import jax.numpy as jnp
from jax import lax
from jax.experimental import pallas as pl
from jax.experimental.pallas import tpu as pltpu
from jax.sharding import PartitionSpec as P

HEAD_DIM = 128
STRETCH = 64
MESH = pl.DeviceIdType.MESH
NT = (((1,), (1,)), ((), ()))
NN = (((1,), (0,)), ((), ()))

norm_eps = 1e-05


def slot_ranks(owners):
    count = owners.shape[0]
    positions = jnp.arange(count)
    same_owner = owners[:, None] == owners[None, :]
    earlier = positions[:, None] > positions[None, :]
    return jnp.sum((same_owner & earlier).astype(jnp.int32), axis=1)


def request_table(owners, slot_rank, slot_ids, shards, capacity):
    matched = (owners[:, None, None] == jnp.arange(shards)[None, :, None]) & (
        slot_rank[:, None, None] == jnp.arange(capacity)[None, None, :]
    )
    return jnp.sum(jnp.where(matched, slot_ids[:, None, None], 0), axis=0)


def kernel(
    shards, sections, capacity, parts, subs,
    wanted, place, gain, hidden, queries, cache, grads, grad_out, weight,
    out,
    req, req_s, cache_v, picked, fetched, q_v, gh_v, wbuf, qg, stage, g_in, hid_in, gout_in,
    load_sem, req_send, req_recv, kv_send, kv_recv, w_send, w_recv, qg_send, qg_recv,
    g_send, g_recv, x_send, x_recv, out_sem,
):
    me = lax.axis_index("stretch")
    sec = lax.axis_index("section")
    before = lax.rem(sec + sections - 1, sections)
    after = lax.rem(sec + 1, sections)
    side = lax.rem(me, 2)
    spot = me // 2
    partner = me + 1 - 2 * side
    line = shards // 2
    tokens, qwidth = queries.shape
    width = hidden.shape[1]
    heads = qwidth // HEAD_DIM
    stretches = tokens // STRETCH
    span = cache.shape[1]
    piece = weight.shape[0] // parts
    chunks = parts * subs
    chunk = piece // subs

    def remote(src, dst, ssem, rsem, stretch, section):
        return pltpu.make_async_remote_copy(
            src_ref=src, dst_ref=dst, send_sem=ssem, recv_sem=rsem,
            device_id=(stretch, section), device_id_type=MESH,
        )

    cache_load = pltpu.make_async_copy(cache, cache_v, load_sem.at[0])
    q_load = pltpu.make_async_copy(queries, q_v, load_sem.at[1])
    gh_load = pltpu.make_async_copy(grads, gh_v, load_sem.at[2])
    cache_load.start()

    barrier = pltpu.get_barrier_semaphore()

    @pl.loop(1, shards)
    def _(off):
        pl.semaphore_signal(
            barrier, inc=1, device_id=(lax.rem(me + off, shards), sec), device_id_type=MESH
        )

    for section in (before, after):
        for stretch in (me, partner):
            pl.semaphore_signal(barrier, inc=1, device_id=(stretch, section), device_id_type=MESH)
    pl.semaphore_wait(barrier, shards + 3)

    def req_copy(to, slot):
        return remote(wanted.at[to], req.at[slot], req_send.at[to], req_recv.at[slot], to, sec)

    @pl.loop(1, shards)
    def _(off):
        req_copy(lax.rem(me + off, shards), me).start()

    q_load.start()
    gh_load.start()
    own_loads = [
        pltpu.make_async_copy(
            weight.at[pl.ds(q * chunk, chunk)], wbuf.at[spot * chunks + q], load_sem.at[4 + q]
        )
        for q in range(chunks)
    ]
    for load in own_loads:
        load.start()
    req[me] = wanted[me]
    cache_load.wait()

    @pl.loop(1, shards)
    def _(off):
        req_copy(lax.rem(me + off, shards), lax.rem(me + off, shards)).wait_recv()

    req_load = pltpu.make_async_copy(req, req_s, load_sem.at[3])
    req_load.start()
    req_load.wait()

    def kv_copy(to, slot):
        return remote(
            picked.at[pl.ds(to * capacity, capacity)],
            fetched.at[pl.ds(slot * capacity, capacity)],
            kv_send.at[to], kv_recv.at[slot], to, sec,
        )

    @pl.loop(1, shards)
    def _(off):
        to = lax.rem(me + off, shards)
        for k in range(capacity):
            picked[to * capacity + k] = cache_v[req_s[to, 0, k]]
        kv_copy(to, me).start()

    for k in range(capacity):
        fetched[me * capacity + k] = cache_v[req_s[me, 0, k]]

    def w_copy(way, block, q):
        unit = block * chunks + q
        return remote(
            wbuf.at[unit], wbuf.at[unit], w_send.at[way, unit], w_recv.at[unit],
            me + (2 if way else -2), sec,
        )

    onward = (spot > 0, spot < line - 1)
    at_end = (
        (spot == line - 1) | (spot == 1), (spot == 0) | (spot == line - 2)
    )

    def first_hop(q, early):
        for way in (0, 1):
            if q == 0:
                go = onward[way]
            elif early:
                go = onward[way] & at_end[way]
            else:
                go = onward[way] & jnp.logical_not(at_end[way])

            @pl.when(go)
            def _():
                w_copy(way, spot, q).start()

    for q in range(chunks):
        own_loads[q].wait()
        first_hop(q, True)

    hid_copy = remote(hidden, hid_in, x_send.at[0], x_recv.at[0], me, before)
    gout_copy = remote(grad_out, gout_in, x_send.at[1], x_recv.at[1], me, before)
    hid_copy.start()
    gout_copy.start()

    def passing(dist, q):
        for way, block in ((1, spot - dist), (0, spot + dist)):
            @pl.when(onward[way] & (block >= 0) & (block < line))
            def _():
                w_copy(way, block, q).wait_recv()
                w_copy(way, block, q).start()

    def ending(dist, q):
        for way, block in ((1, spot - dist), (0, spot + dist)):
            @pl.when(jnp.logical_not(onward[way]) & (block >= 0) & (block < line))
            def _():
                w_copy(way, block, q).wait_recv()

    def rows_from(first, last):
        @pl.loop(first, last)
        def _(off):
            source = lax.rem(me + off, shards)
            kv_copy(source, source).wait_recv()

    passing(1, 0)
    rows_from(1, shards // 2)
    if chunks > 1:
        first_hop(1, False)
    rows_from(shards // 2, shards)
    for q in range(2, chunks):
        first_hop(q, False)

    q_load.wait()
    gh_load.wait()
    factor = HEAD_DIM ** (-0.5)

    def qg_copy(c):
        rows = pl.ds(c * STRETCH, STRETCH)
        return remote(
            qg.at[0, rows], qg.at[1, rows], qg_send.at[c], qg_recv.at[c], partner, sec
        )

    @pl.loop(0, stretches)
    def _(c):
        rows = pl.ds(pl.multiple_of(c * STRETCH, STRETCH), STRETCH)
        first, second = place[c, 0], place[c, 1]
        for h in range(heads):
            cols = slice(h * HEAD_DIM, (h + 1) * HEAD_DIM)
            vcols = slice(qwidth + h * HEAD_DIM, qwidth + (h + 1) * HEAD_DIM)
            keys = jnp.concatenate([fetched[first, :, cols], fetched[second, :, cols]], axis=0)
            values = jnp.concatenate([fetched[first, :, vcols], fetched[second, :, vcols]], axis=0)
            scores = lax.dot_general(
                q_v[rows, cols], keys, NT, preferred_element_type=jnp.float32
            ) * factor
            dprob = lax.dot_general(
                gh_v[rows, cols], values, NT, preferred_element_type=jnp.float32
            )
            exps = jnp.exp(scores - jnp.max(scores, axis=-1, keepdims=True))
            probs = exps / jnp.sum(exps, axis=-1, keepdims=True)
            inner = jnp.sum(probs * dprob, axis=-1, keepdims=True)
            dscore = (factor * probs * (dprob - inner)).astype(jnp.bfloat16)
            qg[0, rows, cols] = lax.dot_general(
                dscore, keys, NN, preferred_element_type=jnp.float32
            ).astype(jnp.bfloat16)
        qg_copy(c).start()
        for q in range(1, chunks):
            @pl.when(c == min(q * stretches // chunks + 1, stretches - 1))
            def _():
                passing(1, q)

    for q in range(subs):
        passing(2, q)

    @pl.loop(0, stretches)
    def _(c):
        qg_copy(c).wait_recv()

    def g_copy(which, block, c):
        unit = (block * 2 + side) * parts + c
        return remote(
            stage.at[which, block * parts + c], g_in.at[unit],
            g_send.at[which, block * parts + c], g_recv.at[unit],
            partner if which else me, before,
        )

    def work(block, c):
        unit = block * parts + c
        rows = wbuf[pl.ds(unit * subs, subs)].reshape(piece, qwidth)
        scale = gain[(block * 2 + side) * parts + c]
        for which in (1, 0):
            product = lax.dot_general(
                qg[which], rows, NT, preferred_element_type=jnp.float32
            )
            stage[which, unit] = (product * scale).astype(jnp.bfloat16)
            g_copy(which, block, c).start()

    @pl.loop(0, line)
    def _(dist):
        @pl.loop(0, parts)
        def _(c):
            for sub in range(subs):
                @pl.when((dist > 0) | (c > 0))
                def _():
                    passing(dist + 2, c * subs + sub)

                @pl.when(dist > 0)
                def _():
                    ending(dist, c * subs + sub)

            @pl.loop(0, 2)
            def _(way):
                block = spot + dist * (2 * way - 1)

                @pl.when((block >= 0) & (block < line) & ((dist > 0) | (way > 0)))
                def _():
                    work(block, c)

    hid_copy.wait_recv()
    gout_copy.wait_recv()
    units = shards * parts

    @pl.loop(0, units)
    def _(unit):
        remote(
            stage.at[0, 0], g_in.at[unit], g_send.at[0, 0], g_recv.at[unit], me, before
        ).wait_recv()

    tile = 32
    tiles = tokens // tile

    def out_copy(i):
        rows = pl.ds(i * tile, tile)
        return pltpu.make_async_copy(gout_in.at[rows], out.at[rows], out_sem.at[i])

    @pl.loop(0, tiles)
    def _(i):
        rows = pl.ds(pl.multiple_of(i * tile, tile), tile)
        squares = jnp.zeros((tile, piece), jnp.float32)
        inners = jnp.zeros((tile, piece), jnp.float32)
        for unit in range(units):
            x = hid_in[rows, unit * piece:(unit + 1) * piece].astype(jnp.float32)
            g = g_in[unit, rows, :].astype(jnp.float32)
            squares += x * x
            inners += g * x
        inv = lax.rsqrt(jnp.sum(squares, axis=-1, keepdims=True) / width + norm_eps)
        mean = jnp.sum(inners, axis=-1, keepdims=True) * inv / width
        slope = inv * inv * mean
        for unit in range(units):
            cols = slice(unit * piece, (unit + 1) * piece)
            x = hid_in[rows, cols].astype(jnp.float32)
            g = g_in[unit, rows, :].astype(jnp.float32)
            total = gout_in[rows, cols].astype(jnp.float32) + (inv * g - slope * x)
            gout_in[rows, cols] = total.astype(jnp.bfloat16)
        out_copy(i).start()

    @pl.loop(1, shards)
    def _(off):
        to = lax.rem(me + off, shards)
        req_copy(to, me).wait_send()
        kv_copy(to, me).wait_send()

    hid_copy.wait_send()
    gout_copy.wait_send()

    @pl.loop(0, stretches)
    def _(c):
        qg_copy(c).wait_send()

    @pl.loop(0, line)
    def _(block):
        for c in range(parts):
            g_copy(0, block, c).wait_send()
            g_copy(1, block, c).wait_send()

        for q in range(chunks):
            @pl.when((block <= spot) & (spot < line - 1))
            def _():
                w_copy(1, block, q).wait_send()

            @pl.when((block >= spot) & (spot > 0))
            def _():
                w_copy(0, block, q).wait_send()

    @pl.loop(0, tiles)
    def _(i):
        out_copy(i).wait()


def local(
    sections, hidden, norm_gain, queries, cache, nbr_shard, nbr_slot, grad_heads, grad_out,
    query_weight,
):
    shards = lax.axis_size("stretch")
    _, tokens, qwidth = queries.shape
    width = hidden.shape[2]
    stretches, neighbours = nbr_shard.shape
    capacity = (neighbours * stretches + shards - 1) // shards
    _, slots, span, _ = cache.shape
    owners = nbr_shard.reshape(-1)
    slot_rank = slot_ranks(owners)
    wanted = request_table(owners, slot_rank, nbr_slot.reshape(-1), shards, capacity)
    wanted = jnp.pad(wanted[:, None, :], ((0, 0), (0, 7), (0, 128 - capacity)))
    place = (owners * capacity + slot_rank).reshape(stretches, neighbours)
    rows = query_weight.shape[1]
    parts = 2 if rows % 512 == 0 else 1
    subs = 2 if rows % 512 == 0 else 1
    piece = rows // parts
    line = shards // 2
    chunks = parts * subs
    units = shards * parts
    bf16 = jnp.bfloat16
    dma = pltpu.SemaphoreType.DMA
    vmem = pl.BlockSpec(memory_space=pltpu.VMEM)
    hbm = pl.BlockSpec(memory_space=pl.ANY)
    out = pl.pallas_call(
        functools.partial(kernel, shards, sections, capacity, parts, subs),
        out_shape=jax.ShapeDtypeStruct((tokens, width), bf16),
        in_specs=[vmem, pl.BlockSpec(memory_space=pltpu.SMEM), vmem] + [hbm] * 6,
        out_specs=hbm,
        scratch_shapes=[
            pltpu.VMEM((shards, 8, 128), jnp.int32),
            pltpu.SMEM((shards, 8, 128), jnp.int32),
            pltpu.VMEM((slots, span, 2 * qwidth), bf16),
            pltpu.VMEM((shards * capacity, span, 2 * qwidth), bf16),
            pltpu.VMEM((shards * capacity, span, 2 * qwidth), bf16),
            pltpu.VMEM((tokens, qwidth), bf16),
            pltpu.VMEM((tokens, qwidth), bf16),
            pltpu.VMEM((line * chunks, piece // subs, qwidth), bf16),
            pltpu.VMEM((2, tokens, qwidth), bf16),
            pltpu.VMEM((2, line * parts, tokens, piece), bf16),
            pltpu.VMEM((units, tokens, piece), bf16),
            pltpu.VMEM((tokens, width), bf16),
            pltpu.VMEM((tokens, width), bf16),
            dma((4 + chunks,)),
            dma((shards,)),
            dma((shards,)),
            dma((shards,)),
            dma((shards,)),
            dma((2, line * chunks)),
            dma((line * chunks,)),
            dma((stretches,)),
            dma((stretches,)),
            dma((2, line * parts)),
            dma((units,)),
            dma((2,)),
            dma((2,)),
            dma((tokens // 32,)),
        ],
        compiler_params=pltpu.CompilerParams(
            collective_id=0, has_side_effects=True, vmem_limit_bytes=60 * 1024 * 1024
        ),
        cost_estimate=pl.CostEstimate(
            flops=2 * tokens * qwidth * width, bytes_accessed=24 << 20, transcendentals=0
        ),
    )(
        wanted, place, norm_gain[0].reshape(units, 1, piece), hidden[0], queries[0], cache[0],
        grad_heads[0], grad_out[0], query_weight[0],
    )
    return out[None]


def solution(mesh):
    in_specs = (
        P("section", "stretch", None),
        P("section", None),
        P("section", "stretch", None),
        P("section", "stretch", None, None),
        P("stretch", None),
        P("stretch", None),
        P("section", "stretch", None),
        P("section", "stretch", None),
        P("section", "stretch", None),
    )
    return jax.shard_map(
        functools.partial(local, mesh.shape["section"]), mesh=mesh, in_specs=in_specs,
        out_specs=P("section", "stretch", None), check_vma=False,
    )
```

```python
import functools

import jax
import jax.numpy as jnp
from jax import lax
from jax.experimental import pallas as pl
from jax.experimental.pallas import tpu as pltpu
from jax.sharding import PartitionSpec as P

HEAD_DIM = 128
STRETCH = 64
MESH = pl.DeviceIdType.MESH
NT = (((1,), (1,)), ((), ()))
NN = (((1,), (0,)), ((), ()))

norm_eps = 1e-05


def slot_ranks(owners):
    count = owners.shape[0]
    positions = jnp.arange(count)
    same_owner = owners[:, None] == owners[None, :]
    earlier = positions[:, None] > positions[None, :]
    return jnp.sum((same_owner & earlier).astype(jnp.int32), axis=1)


def request_table(owners, slot_rank, slot_ids, shards, capacity):
    matched = (owners[:, None, None] == jnp.arange(shards)[None, :, None]) & (
        slot_rank[:, None, None] == jnp.arange(capacity)[None, None, :]
    )
    return jnp.sum(jnp.where(matched, slot_ids[:, None, None], 0), axis=0)


def kernel(
    shards, sections, capacity, parts, subs,
    wanted, place, gain, hidden, queries, cache, grads, grad_out, weight,
    out,
    req, req_s, cache_v, picked, fetched, q_v, gh_v, wbuf, qg, stage, g_in, hid_in, gout_in, sums,
    load_sem, req_send, req_recv, kv_send, kv_recv, w_send, w_recv, qg_send, qg_recv,
    g_send, g_recv, x_send, x_recv, out_sem,
):
    me = lax.axis_index("stretch")
    sec = lax.axis_index("section")
    before = lax.rem(sec + sections - 1, sections)
    after = lax.rem(sec + 1, sections)
    side = lax.rem(me, 2)
    spot = me // 2
    partner = me + 1 - 2 * side
    line = shards // 2
    tokens, qwidth = queries.shape
    width = hidden.shape[1]
    heads = qwidth // HEAD_DIM
    stretches = tokens // STRETCH
    span = cache.shape[1]
    piece = weight.shape[0] // parts
    chunks = parts * subs
    chunk = piece // subs

    def remote(src, dst, ssem, rsem, stretch, section):
        return pltpu.make_async_remote_copy(
            src_ref=src, dst_ref=dst, send_sem=ssem, recv_sem=rsem,
            device_id=(stretch, section), device_id_type=MESH,
        )

    cache_load = pltpu.make_async_copy(cache, cache_v, load_sem.at[0])
    q_load = pltpu.make_async_copy(queries, q_v, load_sem.at[1])
    gh_load = pltpu.make_async_copy(grads, gh_v, load_sem.at[2])
    cache_load.start()

    barrier = pltpu.get_barrier_semaphore()

    @pl.loop(1, shards)
    def _(off):
        pl.semaphore_signal(
            barrier, inc=1, device_id=(lax.rem(me + off, shards), sec), device_id_type=MESH
        )

    for section in (before, after):
        for stretch in (me, partner):
            pl.semaphore_signal(barrier, inc=1, device_id=(stretch, section), device_id_type=MESH)
    pl.semaphore_wait(barrier, shards + 3)

    def req_copy(to, slot):
        return remote(wanted.at[to], req.at[slot], req_send.at[to], req_recv.at[slot], to, sec)

    @pl.loop(1, shards)
    def _(off):
        req_copy(lax.rem(me + off, shards), me).start()

    q_load.start()
    gh_load.start()
    own_loads = [
        pltpu.make_async_copy(
            weight.at[pl.ds(q * chunk, chunk)], wbuf.at[spot * chunks + q], load_sem.at[4 + q]
        )
        for q in range(chunks)
    ]
    for load in own_loads:
        load.start()
    req[me] = wanted[me]
    cache_load.wait()

    @pl.loop(1, shards)
    def _(off):
        req_copy(lax.rem(me + off, shards), lax.rem(me + off, shards)).wait_recv()

    req_load = pltpu.make_async_copy(req, req_s, load_sem.at[3])
    req_load.start()
    req_load.wait()

    def kv_copy(to, slot):
        return remote(
            picked.at[pl.ds(to * capacity, capacity)],
            fetched.at[pl.ds(slot * capacity, capacity)],
            kv_send.at[to], kv_recv.at[slot], to, sec,
        )

    @pl.loop(1, shards)
    def _(off):
        to = lax.rem(me + off, shards)
        for k in range(capacity):
            picked[to * capacity + k] = cache_v[req_s[to, 0, k]]
        kv_copy(to, me).start()

    for k in range(capacity):
        fetched[me * capacity + k] = cache_v[req_s[me, 0, k]]

    def w_copy(way, block, q):
        unit = block * chunks + q
        return remote(
            wbuf.at[unit], wbuf.at[unit], w_send.at[way, unit], w_recv.at[unit],
            me + (2 if way else -2), sec,
        )

    onward = (spot > 0, spot < line - 1)
    at_end = (
        (spot == line - 1) | (spot == 1), (spot == 0) | (spot == line - 2)
    )

    def first_hop(q, early):
        for way in (0, 1):
            if q == 0:
                go = onward[way]
            elif early:
                go = onward[way] & at_end[way]
            else:
                go = onward[way] & jnp.logical_not(at_end[way])

            @pl.when(go)
            def _():
                w_copy(way, spot, q).start()

    for q in range(chunks):
        own_loads[q].wait()
        first_hop(q, True)

    hid_copy = remote(hidden, hid_in, x_send.at[0], x_recv.at[0], me, before)
    gout_copy = remote(grad_out, gout_in, x_send.at[1], x_recv.at[1], me, before)
    hid_copy.start()
    gout_copy.start()

    def passing(dist, q):
        for way, block in ((1, spot - dist), (0, spot + dist)):
            @pl.when(onward[way] & (block >= 0) & (block < line))
            def _():
                w_copy(way, block, q).wait_recv()
                w_copy(way, block, q).start()

    def ending(dist, q):
        for way, block in ((1, spot - dist), (0, spot + dist)):
            @pl.when(jnp.logical_not(onward[way]) & (block >= 0) & (block < line))
            def _():
                w_copy(way, block, q).wait_recv()

    def rows_from(first, last):
        @pl.loop(first, last)
        def _(off):
            source = lax.rem(me + off, shards)
            kv_copy(source, source).wait_recv()

    passing(1, 0)
    rows_from(1, shards // 2)
    if chunks > 1:
        first_hop(1, False)
    rows_from(shards // 2, shards)
    for q in range(2, chunks):
        first_hop(q, False)

    q_load.wait()
    gh_load.wait()
    factor = HEAD_DIM ** (-0.5)

    def qg_copy(c):
        rows = pl.ds(c * STRETCH, STRETCH)
        return remote(
            qg.at[0, rows], qg.at[1, rows], qg_send.at[c], qg_recv.at[c], partner, sec
        )

    @pl.loop(0, stretches)
    def _(c):
        rows = pl.ds(pl.multiple_of(c * STRETCH, STRETCH), STRETCH)
        first, second = place[c, 0], place[c, 1]
        for h in range(heads):
            cols = slice(h * HEAD_DIM, (h + 1) * HEAD_DIM)
            vcols = slice(qwidth + h * HEAD_DIM, qwidth + (h + 1) * HEAD_DIM)
            keys = jnp.concatenate([fetched[first, :, cols], fetched[second, :, cols]], axis=0)
            values = jnp.concatenate([fetched[first, :, vcols], fetched[second, :, vcols]], axis=0)
            scores = lax.dot_general(
                q_v[rows, cols], keys, NT, preferred_element_type=jnp.float32
            ) * factor
            dprob = lax.dot_general(
                gh_v[rows, cols], values, NT, preferred_element_type=jnp.float32
            )
            exps = jnp.exp(scores - jnp.max(scores, axis=-1, keepdims=True))
            probs = exps / jnp.sum(exps, axis=-1, keepdims=True)
            inner = jnp.sum(probs * dprob, axis=-1, keepdims=True)
            dscore = (factor * probs * (dprob - inner)).astype(jnp.bfloat16)
            qg[0, rows, cols] = lax.dot_general(
                dscore, keys, NN, preferred_element_type=jnp.float32
            ).astype(jnp.bfloat16)
        qg_copy(c).start()
        for q in range(1, chunks):
            @pl.when(c == min(q * stretches // chunks + 1, stretches - 1))
            def _():
                passing(1, q)


    def g_copy(which, block, c):
        unit = (block * 2 + side) * parts + c
        return remote(
            stage.at[which, block * parts + c], g_in.at[unit],
            g_send.at[which, block * parts + c], g_recv.at[unit],
            partner if which else me, before,
        )

    def work(block, c):
        unit = block * parts + c
        rows = wbuf[pl.ds(unit * subs, subs)].reshape(piece, qwidth)
        scale = gain[(block * 2 + side) * parts + c]
        for which in (1, 0):
            product = lax.dot_general(
                qg[which], rows, NT, preferred_element_type=jnp.float32
            )
            stage[which, unit] = (product * scale).astype(jnp.bfloat16)
            g_copy(which, block, c).start()

    def shift(q):
        return (-parts, 0, 1, 3)[q] if chunks == 4 else q // subs

    @pl.loop(0, line * parts)
    def _(step):
        dist, c = step // parts, lax.rem(step, parts)
        for q in range(chunks):
            due = step - shift(q)

            @pl.when((due >= parts) & (lax.rem(due, parts) == 0))
            def _():
                passing(due // parts + 1, q)

        @pl.when(step == 0)
        def _():
            @pl.loop(0, stretches)
            def _(c):
                qg_copy(c).wait_recv()

        @pl.when(dist > 0)
        def _():
            for sub in range(subs):
                ending(dist, c * subs + sub)

        @pl.loop(0, 2)
        def _(way):
            block = spot + dist * (2 * way - 1)

            @pl.when((block >= 0) & (block < line) & ((dist > 0) | (way > 0)))
            def _():
                work(block, c)

    hid_copy.wait_recv()
    units = shards * parts
    sums[...] = jnp.zeros_like(sums)

    def add_unit(unit):
        remote(
            stage.at[0, 0], g_in.at[unit], g_send.at[0, 0], g_recv.at[unit], me, before
        ).wait_recv()

        @pl.loop(0, tokens // STRETCH)
        def _(i):
            rows = pl.ds(pl.multiple_of(i * STRETCH, STRETCH), STRETCH)
            squares, inners = sums[0, rows], sums[1, rows]
            for k in range(piece // 128):
                cols = pl.ds(pl.multiple_of(unit * piece + k * 128, 128), 128)
                x = hid_in[rows, cols].astype(jnp.float32)
                g = g_in[unit, rows, k * 128:(k + 1) * 128].astype(jnp.float32)
                squares += x * x
                inners += g * x
            sums[0, rows] = squares
            sums[1, rows] = inners

    @pl.loop(0, line * parts)
    def _(step):
        dist, c = step // parts, lax.rem(step, parts)

        @pl.loop(0, 4)
        def _(k):
            way, half = k // 2, lax.rem(k, 2)
            block = spot + dist * (2 * way - 1)

            @pl.when((block >= 0) & (block < line) & ((dist > 0) | (way > 0)))
            def _():
                add_unit((block * 2 + half) * parts + c)

    gout_copy.wait_recv()
    tile = 32
    tiles = tokens // tile

    def out_copy(i):
        rows = pl.ds(i * tile, tile)
        return pltpu.make_async_copy(gout_in.at[rows], out.at[rows], out_sem.at[i])

    @pl.loop(0, tiles)
    def _(i):
        rows = pl.ds(pl.multiple_of(i * tile, tile), tile)
        inv = lax.rsqrt(jnp.sum(sums[0, rows], axis=-1, keepdims=True) / width + norm_eps)
        mean = jnp.sum(sums[1, rows], axis=-1, keepdims=True) * inv / width
        slope = inv * inv * mean
        for unit in range(units):
            cols = slice(unit * piece, (unit + 1) * piece)
            x = hid_in[rows, cols].astype(jnp.float32)
            g = g_in[unit, rows, :].astype(jnp.float32)
            total = gout_in[rows, cols].astype(jnp.float32) + (inv * g - slope * x)
            gout_in[rows, cols] = total.astype(jnp.bfloat16)
        out_copy(i).start()

    @pl.loop(1, shards)
    def _(off):
        to = lax.rem(me + off, shards)
        req_copy(to, me).wait_send()
        kv_copy(to, me).wait_send()

    hid_copy.wait_send()
    gout_copy.wait_send()

    @pl.loop(0, stretches)
    def _(c):
        qg_copy(c).wait_send()

    @pl.loop(0, line)
    def _(block):
        for c in range(parts):
            g_copy(0, block, c).wait_send()
            g_copy(1, block, c).wait_send()

        for q in range(chunks):
            @pl.when((block <= spot) & (spot < line - 1))
            def _():
                w_copy(1, block, q).wait_send()

            @pl.when((block >= spot) & (spot > 0))
            def _():
                w_copy(0, block, q).wait_send()

    @pl.loop(0, tiles)
    def _(i):
        out_copy(i).wait()


def local(
    sections, hidden, norm_gain, queries, cache, nbr_shard, nbr_slot, grad_heads, grad_out,
    query_weight,
):
    shards = lax.axis_size("stretch")
    _, tokens, qwidth = queries.shape
    width = hidden.shape[2]
    stretches, neighbours = nbr_shard.shape
    capacity = (neighbours * stretches + shards - 1) // shards
    _, slots, span, _ = cache.shape
    owners = nbr_shard.reshape(-1)
    slot_rank = slot_ranks(owners)
    wanted = request_table(owners, slot_rank, nbr_slot.reshape(-1), shards, capacity)
    wanted = jnp.pad(wanted[:, None, :], ((0, 0), (0, 7), (0, 128 - capacity)))
    place = (owners * capacity + slot_rank).reshape(stretches, neighbours)
    rows = query_weight.shape[1]
    parts = 2 if rows % 512 == 0 else 1
    subs = 2 if rows % 512 == 0 else 1
    piece = rows // parts
    line = shards // 2
    chunks = parts * subs
    units = shards * parts
    bf16 = jnp.bfloat16
    dma = pltpu.SemaphoreType.DMA
    vmem = pl.BlockSpec(memory_space=pltpu.VMEM)
    hbm = pl.BlockSpec(memory_space=pl.ANY)
    out = pl.pallas_call(
        functools.partial(kernel, shards, sections, capacity, parts, subs),
        out_shape=jax.ShapeDtypeStruct((tokens, width), bf16),
        in_specs=[vmem, pl.BlockSpec(memory_space=pltpu.SMEM), vmem] + [hbm] * 6,
        out_specs=hbm,
        scratch_shapes=[
            pltpu.VMEM((shards, 8, 128), jnp.int32),
            pltpu.SMEM((shards, 8, 128), jnp.int32),
            pltpu.VMEM((slots, span, 2 * qwidth), bf16),
            pltpu.VMEM((shards * capacity, span, 2 * qwidth), bf16),
            pltpu.VMEM((shards * capacity, span, 2 * qwidth), bf16),
            pltpu.VMEM((tokens, qwidth), bf16),
            pltpu.VMEM((tokens, qwidth), bf16),
            pltpu.VMEM((line * chunks, piece // subs, qwidth), bf16),
            pltpu.VMEM((2, tokens, qwidth), bf16),
            pltpu.VMEM((2, line * parts, tokens, piece), bf16),
            pltpu.VMEM((units, tokens, piece), bf16),
            pltpu.VMEM((tokens, width), bf16),
            pltpu.VMEM((tokens, width), bf16),
            pltpu.VMEM((2, tokens, 128), jnp.float32),
            dma((4 + chunks,)),
            dma((shards,)),
            dma((shards,)),
            dma((shards,)),
            dma((shards,)),
            dma((2, line * chunks)),
            dma((line * chunks,)),
            dma((stretches,)),
            dma((stretches,)),
            dma((2, line * parts)),
            dma((units,)),
            dma((2,)),
            dma((2,)),
            dma((tokens // 32,)),
        ],
        compiler_params=pltpu.CompilerParams(
            collective_id=0, has_side_effects=True, vmem_limit_bytes=60 * 1024 * 1024
        ),
        cost_estimate=pl.CostEstimate(
            flops=2 * tokens * qwidth * width, bytes_accessed=24 << 20, transcendentals=0
        ),
    )(
        wanted, place, norm_gain[0].reshape(units, 1, piece), hidden[0], queries[0], cache[0],
        grad_heads[0], grad_out[0], query_weight[0],
    )
    return out[None]


def solution(mesh):
    in_specs = (
        P("section", "stretch", None),
        P("section", None),
        P("section", "stretch", None),
        P("section", "stretch", None, None),
        P("stretch", None),
        P("stretch", None),
        P("section", "stretch", None),
        P("section", "stretch", None),
        P("section", "stretch", None),
    )
    return jax.shard_map(
        functools.partial(local, mesh.shape["section"]), mesh=mesh, in_specs=in_specs,
        out_specs=P("section", "stretch", None), check_vma=False,
    )
```
